32 devices in a mesh: dp: 8 (over z, core), expert: 4 (over y, x).
Axes of the slice: x: 2, y: 2, z: 4, core: 2. Of those that a mesh axis runs over, the one named last changes fastest.
Arguments:
- tokens: bfloat16 [4, 1024, 3584], P('expert', 'dp'), may hold values from -6 to 6
- grad_out: bfloat16 [4, 1024, 3584], P('expert', 'dp'), may hold values from -6 to 6
- route_ids: int32 [4, 1024], P('expert', 'dp'), may hold values from 0 to 3, as said below
- route_gates: float32 [4, 1024], P('expert', 'dp'), may hold values from 0.2 to 1
- w_gate: bfloat16 [4, 3584, 1024], P('expert', 'dp'), may hold values from -0.09375 to 0.09375
- w_up: bfloat16 [4, 3584, 1024], P('expert', 'dp'), may hold values from -0.09375 to 0.09375
- w_down: bfloat16 [4, 1024, 3584], P('expert', 'dp'), may hold values from -0.1875 to 0.1875
Outputs:
- moe_out: bfloat16 [4, 1024, 3584], P('expert', 'dp')
- input_grad: bfloat16 [4, 1024, 3584], P('expert', None, 'dp')
- gate_grad: float32 [4, 1024], P('expert', 'dp')
The draws below stay inside these ranges and needn't reach their ends.
Inputs may be any that keep to these rules, and one draw needn't show every extreme that they name: `route_ids`: among the 128 tokens of one device at most 80 name the same expert; one expert is named by exactly 80 tokens of every device; on one device the counts of the other experts differ by at most one.
All inputs are finite; a program needn't handle non-finite values.
Results may differ from the reference program's by a relative error of at most 0.0057.
Values may be sent and summed in bfloat16 or wider, within the bound.
A program may use at most 128 MiB of HBM per device.

```python
import math
import jax
import jax.numpy as jnp
from jax import lax

D = 3584
FF = 1024
TOK_DEV = 128
EXPERTS = 4
CAP = 80
BATCH = 4
LENGTH = 1024


def draw_route_ids(key, part):
    block_count = BATCH * (LENGTH // TOK_DEV)
    hot_key = jax.random.fold_in(key, 11)
    order_key = jax.random.fold_in(key, 12)
    offset_key = jax.random.fold_in(key, 13)
    hot_expert = jax.random.randint(hot_key, (), 0, EXPERTS, dtype=jnp.int32)
    block_keys = jax.random.split(order_key, block_count)
    ranks = jax.vmap(lambda block_key: jax.random.permutation(block_key, TOK_DEV))(block_keys).astype(jnp.int32)
    offsets = jax.random.randint(offset_key, (block_count, 1), 0, EXPERTS - 1, dtype=jnp.int32)
    others = (ranks - CAP + offsets) % (EXPERTS - 1)
    others = others + (others >= hot_expert).astype(jnp.int32)
    chosen = jnp.where(ranks < CAP, hot_expert, others)
    return chosen.reshape(BATCH, LENGTH).astype(jnp.int32)


def level_of(stream_key, shape, cuts, least, largest):
    def one(axis_at, parts):
        heights = jax.random.uniform(jax.random.fold_in(jax.random.fold_in(stream_key, 6), axis_at), (parts,), jnp.float32, least / len(cuts), largest / len(cuts))
        return jnp.repeat(jnp.exp(heights), shape[axis_at] // parts).reshape((-1,) + (1,) * (len(shape) - axis_at - 1))

    loudness = one(*cuts[0])
    for cut in cuts[1:]:
        loudness = loudness * one(*cut)
    return loudness


def normal_values(own_key, shape, deviation, bound, shards=(), kind=jnp.bfloat16):
    drawn = deviation * jax.random.normal(own_key, shape, jnp.float32)
    if shards:
        drawn = drawn * level_of(own_key, shape, shards, -0.22, 0.18)
    return jnp.clip(drawn, -bound, bound).astype(kind)


def setup_inputs(seed: int = 0) -> dict:
    key_of = jax.random.split(jax.random.key(seed), 8)
    return {
        "tokens": normal_values(key_of[0], (BATCH, LENGTH, D), 1.0, 6.0, ((0, 4), (1, 8))),
        "grad_out": normal_values(key_of[1], (BATCH, LENGTH, D), 1.0, 6.0, ((0, 4), (1, 8))),
        "route_ids": draw_route_ids(jax.random.fold_in(key_of[7], 71), 0),
        "route_gates": jnp.clip(jnp.exp(math.log(1.0) - 1.609438 * jax.random.uniform(key_of[3], (BATCH, LENGTH), jnp.float32) ** level_of(key_of[3], (BATCH, LENGTH), ((0, 4), (1, 8)), -0.2, 0.2)), 0.2, 1.0),
        "w_gate": normal_values(key_of[4], (EXPERTS, D, FF), D ** -0.5, 0.09375, ((0, 4), (1, 8))),
        "w_up": normal_values(key_of[5], (EXPERTS, D, FF), D ** -0.5, 0.09375, ((0, 4), (1, 8))),
        "w_down": normal_values(key_of[6], (EXPERTS, FF, D), FF ** -0.5, 0.1875, ((0, 4), (1, 8))),
    }


def expert_pass(routed, routed_grad, gate_matrix, up_matrix, down_matrix):
    gate_pre = jnp.dot(routed, gate_matrix, preferred_element_type=jnp.float32)
    up_pre = jnp.dot(routed, up_matrix, preferred_element_type=jnp.float32)
    sigmoid_gate = jax.nn.sigmoid(gate_pre)
    silu_gate = gate_pre * sigmoid_gate
    hidden = (silu_gate * up_pre).astype(jnp.bfloat16)
    expert_out = jnp.dot(hidden, down_matrix, preferred_element_type=jnp.float32).astype(jnp.bfloat16)
    hidden_grad = jnp.dot(routed_grad, down_matrix.T, preferred_element_type=jnp.float32)
    gate_pre_grad = (hidden_grad * up_pre * sigmoid_gate * (1.0 + gate_pre * (1.0 - sigmoid_gate))).astype(jnp.bfloat16)
    up_pre_grad = (hidden_grad * silu_gate).astype(jnp.bfloat16)
    input_rows = jnp.dot(gate_pre_grad, gate_matrix.T, preferred_element_type=jnp.float32)
    input_rows = input_rows + jnp.dot(up_pre_grad, up_matrix.T, preferred_element_type=jnp.float32)
    return expert_out, input_rows.astype(jnp.bfloat16)


def reference(tokens, grad_out, route_ids, route_gates, w_gate, w_up, w_down):
    width = tokens.shape[-1]
    flat_tokens = tokens.reshape(-1, width)
    flat_grad = grad_out.reshape(-1, width)
    flat_ids = route_ids.reshape(-1).astype(jnp.int32)
    flat_gates = route_gates.reshape(-1)
    scaled_grad = (flat_gates[:, None] * flat_grad.astype(jnp.float32)).astype(jnp.bfloat16)
    row_total = flat_ids.shape[0]
    block_rows = 512
    block_count = (row_total + block_rows - 1) // block_rows
    padded_total = block_count * block_rows
    order = jnp.argsort(flat_ids, stable=True).astype(jnp.int32)
    order = jnp.concatenate([order, jnp.full((padded_total - row_total,), order[-1], jnp.int32)])
    sorted_ids = flat_ids[order].reshape(block_count, block_rows)
    sorted_tokens = flat_tokens[order].reshape(block_count, block_rows, width)
    sorted_grad = scaled_grad[order].reshape(block_count, block_rows, width)

    def one_block(block_args):
        block_ids, block_tokens, block_grad = block_args

        def one_expert(expert, carry):
            out_total, input_total = carry
            expert_out, input_rows = expert_pass(block_tokens, block_grad, w_gate[expert], w_up[expert], w_down[expert])
            chosen = (block_ids == expert)[:, None]
            return jnp.where(chosen, expert_out, out_total), jnp.where(chosen, input_rows, input_total)

        start_carry = (jnp.zeros_like(block_tokens), jnp.zeros_like(block_tokens))
        return lax.fori_loop(block_ids[0], block_ids[-1] + 1, one_expert, start_carry)

    out_sorted, input_sorted = lax.map(one_block, (sorted_ids, sorted_tokens, sorted_grad))
    expert_out = jnp.zeros_like(flat_tokens).at[order].set(out_sorted.reshape(padded_total, width))
    input_grad = jnp.zeros_like(flat_tokens).at[order].set(input_sorted.reshape(padded_total, width))
    moe_out = (flat_gates[:, None] * expert_out.astype(jnp.float32)).astype(jnp.bfloat16)
    gate_grad = jnp.sum(flat_grad.astype(jnp.float32) * expert_out.astype(jnp.float32), axis=-1)
    return moe_out.reshape(tokens.shape), input_grad.reshape(tokens.shape), gate_grad.reshape(route_gates.shape)
```

```python
import jax
import jax.numpy as jnp
from jax import lax
from jax.sharding import PartitionSpec as P

F32 = jnp.float32
BF16 = jnp.bfloat16
DOWN_PARTS = 2


def placement(route_line, expert_count, capacity):
    tok_count = route_line.shape[0]
    same = route_line[:, None] == route_line[None, :]
    earlier = jnp.arange(tok_count)[None, :] < jnp.arange(tok_count)[:, None]
    placed = jnp.sum((same & earlier).astype(jnp.int32), axis=1)
    slots = route_line * capacity + placed
    rows = jnp.arange(expert_count * capacity, dtype=jnp.int32)
    return (rows[:, None] == slots[None, :]).astype(BF16)


def mm(a, b, dims=(((1,), (0,)), ((), ()))):
    return lax.dot_general(a, b, dims, preferred_element_type=F32)


NT = (((1,), (1,)), ((), ()))
TN = (((0,), (0,)), ((), ()))


def local(tokens, grad_out, route_ids, route_gates, w_gate, w_up, w_down):
    expert_count = lax.axis_size("expert")
    dp_count = lax.axis_size("dp")
    tok_count = tokens.shape[1]
    width = tokens.shape[2]
    capacity = max(2, 5 * tok_count // (2 * expert_count))
    place = placement(route_ids[0], expert_count, capacity)
    own_grad = grad_out[0].astype(F32)
    gate_column = route_gates[0][:, None]
    scaled_grad = (gate_column * own_grad).astype(BF16)

    def over_experts(rows):
        cols = rows.shape[1]
        got = lax.all_to_all(
            rows.reshape(expert_count, capacity, cols),
            "expert", split_axis=0, concat_axis=0, tiled=True,
        )
        return got.reshape(expert_count * capacity, cols)

    gate_matrix = lax.all_gather(w_gate, "dp", axis=1, tiled=True)[0]
    up_matrix = lax.all_gather(w_up, "dp", axis=1, tiled=True)[0]
    w_down, _ = lax.optimization_barrier((w_down, gate_matrix[:16, :128]))
    step = width // DOWN_PARTS
    spans = [slice(i * step, (i + 1) * step) for i in range(DOWN_PARTS)]
    downs = [lax.all_gather(w_down[:, :, s], "dp", axis=1, tiled=True)[0] for s in spans]

    routed = over_experts(mm(place, tokens[0]).astype(BF16))
    routed_grad = over_experts(mm(place, scaled_grad).astype(BF16))

    gate_pre = mm(routed, gate_matrix)
    up_pre = mm(routed, up_matrix)
    sigmoid_gate = jax.nn.sigmoid(gate_pre)
    silu_gate = gate_pre * sigmoid_gate
    hidden = (silu_gate * up_pre).astype(BF16)

    moe_parts = []
    gate_grad = jnp.zeros((tok_count,), F32)
    hidden_grad = jnp.zeros_like(gate_pre)
    for s, down in zip(spans, downs):
        expert_out = mm(hidden, down).astype(BF16)
        hidden_grad = hidden_grad + mm(routed_grad[:, s], down, NT)
        token_out = mm(place, over_experts(expert_out), TN)
        moe_parts.append((gate_column * token_out).astype(BF16))
        gate_grad = gate_grad + jnp.sum(own_grad[:, s] * token_out, axis=1)
    moe_out = jnp.concatenate(moe_parts, axis=1)

    gate_pre_grad = (
        hidden_grad * up_pre * sigmoid_gate * (1.0 + gate_pre * (1.0 - sigmoid_gate))
    ).astype(BF16)
    up_pre_grad = (hidden_grad * silu_gate).astype(BF16)
    input_rows = (mm(gate_pre_grad, gate_matrix, NT) + mm(up_pre_grad, up_matrix, NT)).astype(BF16)
    home_rows = over_experts(input_rows)
    token_grad = mm(home_rows, place, TN).astype(BF16)
    parts = token_grad.reshape(dp_count, width // dp_count, tok_count)
    heads = lax.all_to_all(parts, "dp", split_axis=0, concat_axis=0, tiled=True)
    input_grad = heads.transpose(0, 2, 1).reshape(1, dp_count * tok_count, width // dp_count)
    return (moe_out[None], input_grad, gate_grad[None])


def solution(mesh):
    in_specs = (
        P("expert", "dp", None),
        P("expert", "dp", None),
        P("expert", "dp"),
        P("expert", "dp"),
        P("expert", "dp", None),
        P("expert", "dp", None),
        P("expert", "dp", None),
    )
    out_specs = (P("expert", "dp", None), P("expert", None, "dp"), P("expert", "dp"))
    return jax.shard_map(local, mesh=mesh, in_specs=in_specs, out_specs=out_specs, check_vma=False)
```

```python
import functools

import jax
import jax.numpy as jnp
from jax import lax
from jax.experimental import pallas as pl
from jax.experimental.pallas import tpu as pltpu
from jax.sharding import PartitionSpec as P

F32 = jnp.float32
BF16 = jnp.bfloat16


def gather_kernel(dp_count, *refs):
    count = (len(refs) - 5) // 2
    shards, wholes = refs[:count], refs[count : 2 * count]
    right_sem, left_sem, pair_sem, recv_sem, own_sem = refs[2 * count :]
    line = dp_count // 2
    me = lax.axis_index("dp")
    z, core = me // 2, me % 2
    pair = z * 2 + (1 - core)
    has_left, has_right = z > 0, z < line - 1

    def greet(target):
        pl.semaphore_signal(
            barrier, inc=1, device_id={"dp": target}, device_id_type=pl.DeviceIdType.MESH
        )

    barrier = pltpu.get_barrier_semaphore()
    greet(pair)
    pl.when(has_left)(lambda: greet(me - 2))
    pl.when(has_right)(lambda: greet(me + 2))
    pl.semaphore_wait(barrier, 1 + has_left.astype(jnp.int32) + has_right.astype(jnp.int32))

    def block(w, slot):
        rows = shards[w].shape[0]
        return wholes[w].at[pl.ds(pl.multiple_of(slot * rows, rows), rows)]

    def copy(w, slot, sems, step, target, own=False):
        return pltpu.make_async_remote_copy(
            src_ref=shards[w] if own else block(w, slot),
            dst_ref=block(w, slot),
            send_sem=sems.at[w, step],
            recv_sem=recv_sem.at[w, slot],
            device_id={"dp": target},
            device_id_type=pl.DeviceIdType.MESH,
        )

    for w in range(count):
        pl.when(has_right)(lambda: copy(w, me, right_sem, 0, me + 2, True).start())
        pl.when(has_left)(lambda: copy(w, me, left_sem, 0, me - 2, True).start())
        copy(w, me, pair_sem, z, pair, True).start()
        pltpu.make_async_copy(shards[w], block(w, me), own_sem.at[w]).start()

    for step in range(1, line):
        for w in range(count):
            @pl.when(z >= step)
            def _():
                slot = me - 2 * step
                copy(w, slot, pair_sem, z - step, pair).wait_recv()
                pl.when(has_right)(lambda: copy(w, slot, right_sem, step, me + 2).start())
                copy(w, slot, pair_sem, z - step, pair).start()

            @pl.when(z + step < line)
            def _():
                slot = me + 2 * step
                copy(w, slot, pair_sem, z + step, pair).wait_recv()
                pl.when(has_left)(lambda: copy(w, slot, left_sem, step, me - 2).start())
                copy(w, slot, pair_sem, z + step, pair).start()

    for w in range(count):
        pltpu.make_async_copy(shards[w], block(w, me), own_sem.at[w]).wait()
        for other in range(line):
            copy(w, other * 2 + 1 - core, pair_sem, other, pair).wait_recv()
            copy(w, other * 2 + core, pair_sem, other, pair).wait_send()
        for step in range(line):
            pl.when(has_right & (z >= step))(
                lambda: copy(w, me - 2 * step, right_sem, step, me + 2).wait_send()
            )
            pl.when(has_left & (z + step < line))(
                lambda: copy(w, me + 2 * step, left_sem, step, me - 2).wait_send()
            )


def gather_weights(dp_count, shards):
    count, line = len(shards), dp_count // 2
    hbm = pl.BlockSpec(memory_space=pl.ANY)
    moved = sum(x.size for x in shards) * 2 * dp_count
    return pl.pallas_call(
        functools.partial(gather_kernel, dp_count),
        out_shape=[
            jax.ShapeDtypeStruct((dp_count * x.shape[0], x.shape[1]), x.dtype) for x in shards
        ],
        in_specs=[hbm] * count,
        out_specs=[hbm] * count,
        scratch_shapes=[
            pltpu.SemaphoreType.DMA((count, line)),
            pltpu.SemaphoreType.DMA((count, line)),
            pltpu.SemaphoreType.DMA((count, line)),
            pltpu.SemaphoreType.DMA((count, dp_count)),
            pltpu.SemaphoreType.DMA((count,)),
        ],
        cost_estimate=pl.CostEstimate(flops=0, bytes_accessed=moved * 25, transcendentals=0),
        compiler_params=pltpu.CompilerParams(collective_id=3, has_side_effects=True),
    )(*shards)


def placement(route_line, expert_count, capacity):
    tok_count = route_line.shape[0]
    same = route_line[:, None] == route_line[None, :]
    earlier = jnp.arange(tok_count)[None, :] < jnp.arange(tok_count)[:, None]
    placed = jnp.sum((same & earlier).astype(jnp.int32), axis=1)
    slots = route_line * capacity + placed
    rows = jnp.arange(expert_count * capacity, dtype=jnp.int32)
    return (rows[:, None] == slots[None, :]).astype(BF16)


def mm(a, b, dims=(((1,), (0,)), ((), ()))):
    return lax.dot_general(a, b, dims, preferred_element_type=F32)


NT = (((1,), (1,)), ((), ()))
TN = (((0,), (0,)), ((), ()))


def local(tokens, grad_out, route_ids, route_gates, w_gate, w_up, w_down):
    expert_count = lax.axis_size("expert")
    dp_count = lax.axis_size("dp")
    tok_count = tokens.shape[1]
    width = tokens.shape[2]
    capacity = max(2, 5 * tok_count // (2 * expert_count))
    place = placement(route_ids[0], expert_count, capacity)
    own_grad = grad_out[0].astype(F32)
    gate_column = route_gates[0][:, None]
    scaled_grad = (gate_column * own_grad).astype(BF16)

    def over_experts(rows):
        cols = rows.shape[1]
        got = lax.all_to_all(
            rows.reshape(expert_count, capacity, cols),
            "expert", split_axis=0, concat_axis=0, tiled=True,
        )
        return got.reshape(expert_count * capacity, cols)

    send = jnp.concatenate(
        [
            mm(place, rows).astype(BF16).reshape(expert_count, capacity, width)
            for rows in (tokens[0], scaled_grad)
        ],
        axis=1,
    )
    arrived = lax.all_to_all(send, "expert", split_axis=0, concat_axis=0, tiled=True)
    routed = arrived[:, :capacity].reshape(expert_count * capacity, width)
    routed_grad = arrived[:, capacity:].reshape(expert_count * capacity, width)

    gate_matrix, up_matrix, down_matrix = gather_weights(
        dp_count, (w_gate[0], w_up[0], w_down[0])
    )

    gate_pre = mm(routed, gate_matrix)
    up_pre = mm(routed, up_matrix)
    sigmoid_gate = jax.nn.sigmoid(gate_pre)
    silu_gate = gate_pre * sigmoid_gate
    hidden = (silu_gate * up_pre).astype(BF16)
    expert_out = mm(hidden, down_matrix).astype(BF16)
    hidden_grad = mm(routed_grad, down_matrix, NT)
    expert_out, hidden_grad = lax.optimization_barrier((expert_out, hidden_grad))
    returned = over_experts(expert_out)

    gate_pre_grad = (
        hidden_grad * up_pre * sigmoid_gate * (1.0 + gate_pre * (1.0 - sigmoid_gate))
    ).astype(BF16)
    up_pre_grad = (hidden_grad * silu_gate).astype(BF16)
    input_rows = (mm(gate_pre_grad, gate_matrix, NT) + mm(up_pre_grad, up_matrix, NT)).astype(BF16)
    input_rows, returned = lax.optimization_barrier((input_rows, returned))
    home_rows = over_experts(input_rows)
    token_out = mm(place, returned, TN)
    moe_out = (gate_column * token_out).astype(BF16)
    gate_grad = jnp.sum(own_grad * token_out, axis=1)
    token_grad = mm(home_rows, place, TN).astype(BF16)
    parts = token_grad.reshape(dp_count, width // dp_count, tok_count)
    heads = lax.all_to_all(parts, "dp", split_axis=0, concat_axis=0, tiled=True)
    input_grad = heads.transpose(0, 2, 1).reshape(1, dp_count * tok_count, width // dp_count)
    return (moe_out[None], input_grad, gate_grad[None])


def solution(mesh):
    in_specs = (
        P("expert", "dp", None),
        P("expert", "dp", None),
        P("expert", "dp"),
        P("expert", "dp"),
        P("expert", "dp", None),
        P("expert", "dp", None),
        P("expert", "dp", None),
    )
    out_specs = (P("expert", "dp", None), P("expert", None, "dp"), P("expert", "dp"))
    return jax.shard_map(local, mesh=mesh, in_specs=in_specs, out_specs=out_specs, check_vma=False)
```

```python
import functools

import jax
import jax.numpy as jnp
from jax import lax
from jax.experimental import pallas as pl
from jax.experimental.pallas import tpu as pltpu
from jax.sharding import PartitionSpec as P

F32 = jnp.float32
BF16 = jnp.bfloat16


def gather_kernel(dp_count, *refs):
    count = (len(refs) - 5) // 2
    shards, wholes = refs[:count], refs[count : 2 * count]
    right_sem, left_sem, pair_sem, recv_sem, own_sem = refs[2 * count :]
    line = dp_count // 2
    me = lax.axis_index("dp")
    z, core = me // 2, me % 2
    pair = z * 2 + (1 - core)
    has_left, has_right = z > 0, z < line - 1

    def greet(target):
        pl.semaphore_signal(
            barrier, inc=1, device_id={"dp": target}, device_id_type=pl.DeviceIdType.MESH
        )

    barrier = pltpu.get_barrier_semaphore()
    greet(pair)
    pl.when(has_left)(lambda: greet(me - 2))
    pl.when(has_right)(lambda: greet(me + 2))
    pl.semaphore_wait(barrier, 1 + has_left.astype(jnp.int32) + has_right.astype(jnp.int32))

    def block(w, slot):
        rows = shards[w].shape[0]
        return wholes[w].at[pl.ds(pl.multiple_of(slot * rows, rows), rows)]

    def copy(w, slot, sems, step, target, own=False):
        return pltpu.make_async_remote_copy(
            src_ref=shards[w] if own else block(w, slot),
            dst_ref=block(w, slot),
            send_sem=sems.at[w, step],
            recv_sem=recv_sem.at[w, slot],
            device_id={"dp": target},
            device_id_type=pl.DeviceIdType.MESH,
        )

    for w in range(count):
        pl.when(has_right)(lambda: copy(w, me, right_sem, 0, me + 2, True).start())
        pl.when(has_left)(lambda: copy(w, me, left_sem, 0, me - 2, True).start())
        copy(w, me, pair_sem, z, pair, True).start()
        pltpu.make_async_copy(shards[w], block(w, me), own_sem.at[w]).start()

    for step in range(1, line):
        for w in range(count):
            @pl.when(z >= step)
            def _():
                slot = me - 2 * step
                copy(w, slot, pair_sem, z - step, pair).wait_recv()
                pl.when(has_right)(lambda: copy(w, slot, right_sem, step, me + 2).start())
                copy(w, slot, pair_sem, z - step, pair).start()

            @pl.when(z + step < line)
            def _():
                slot = me + 2 * step
                copy(w, slot, pair_sem, z + step, pair).wait_recv()
                pl.when(has_left)(lambda: copy(w, slot, left_sem, step, me - 2).start())
                copy(w, slot, pair_sem, z + step, pair).start()

    for w in range(count):
        pltpu.make_async_copy(shards[w], block(w, me), own_sem.at[w]).wait()
        for other in range(line):
            copy(w, other * 2 + 1 - core, pair_sem, other, pair).wait_recv()
            copy(w, other * 2 + core, pair_sem, other, pair).wait_send()
        for step in range(line):
            pl.when(has_right & (z >= step))(
                lambda: copy(w, me - 2 * step, right_sem, step, me + 2).wait_send()
            )
            pl.when(has_left & (z + step < line))(
                lambda: copy(w, me + 2 * step, left_sem, step, me - 2).wait_send()
            )


def gather_weights(dp_count, shards):
    count, line = len(shards), dp_count // 2
    hbm = pl.BlockSpec(memory_space=pl.ANY)
    moved = sum(x.size for x in shards) * 2 * dp_count
    return pl.pallas_call(
        functools.partial(gather_kernel, dp_count),
        out_shape=[
            jax.ShapeDtypeStruct((dp_count * x.shape[0], x.shape[1]), x.dtype) for x in shards
        ],
        in_specs=[hbm] * count,
        out_specs=[hbm] * count,
        scratch_shapes=[
            pltpu.SemaphoreType.DMA((count, line)),
            pltpu.SemaphoreType.DMA((count, line)),
            pltpu.SemaphoreType.DMA((count, line)),
            pltpu.SemaphoreType.DMA((count, dp_count)),
            pltpu.SemaphoreType.DMA((count,)),
        ],
        cost_estimate=pl.CostEstimate(flops=0, bytes_accessed=moved * 25, transcendentals=0),
        compiler_params=pltpu.CompilerParams(collective_id=3, has_side_effects=True),
    )(*shards)


def placement(route_line, expert_count, capacity):
    tok_count = route_line.shape[0]
    same = route_line[:, None] == route_line[None, :]
    earlier = jnp.arange(tok_count)[None, :] < jnp.arange(tok_count)[:, None]
    placed = jnp.sum((same & earlier).astype(jnp.int32), axis=1)
    slots = route_line * capacity + placed
    rows = jnp.arange(expert_count * capacity, dtype=jnp.int32)
    return (rows[:, None] == slots[None, :]).astype(BF16)


def mm(a, b, dims=(((1,), (0,)), ((), ()))):
    return lax.dot_general(a, b, dims, preferred_element_type=F32)


NT = (((1,), (1,)), ((), ()))
TN = (((0,), (0,)), ((), ()))


def heads_kernel(expert_count, dp_count, rows, place, out, got, turned, *sems):
    row_sem, got_sem, own_sem, turn_sem, head_sem, keep_sem = sems
    expert, me = lax.axis_index("expert"), lax.axis_index("dp")
    chunks, cols = got.shape[0], got.shape[3]
    depth, tok_count = out.shape[0], place.shape[2]
    per = cols // depth
    mesh_type = pl.DeviceIdType.MESH

    barrier = pltpu.get_barrier_semaphore()
    for o in range(1, expert_count):
        pl.semaphore_signal(
            barrier, inc=1, device_id={"expert": (expert + o) % expert_count},
            device_id_type=mesh_type,
        )
    for o in range(1, dp_count):
        pl.semaphore_signal(
            barrier, inc=1, device_id={"dp": (me + o) % dp_count}, device_id_type=mesh_type
        )
    pl.semaphore_wait(barrier, expert_count + dp_count - 2)

    def chunk_of(i):
        return (me // per + 1 + i) % chunks

    def source(k, e):
        return rows.at[e, :, pl.ds(pl.multiple_of(k * cols, 128), cols)]

    def give(i, target, slot):
        k = chunk_of(i)
        return pltpu.make_async_remote_copy(
            src_ref=source(k, target), dst_ref=got.at[k, slot],
            send_sem=row_sem.at[i, target], recv_sem=got_sem.at[i, slot],
            device_id={"expert": target}, device_id_type=mesh_type,
        )

    def keep(i):
        k = chunk_of(i)
        return pltpu.make_async_copy(source(k, expert), got.at[k, expert], own_sem.at[i])

    def column(slot):
        return out.at[:, pl.ds(pl.multiple_of(slot * tok_count, 128), tok_count)]

    def hand(i, p, target, slot):
        return pltpu.make_async_remote_copy(
            src_ref=turned.at[i, pl.ds(p * depth, depth)], dst_ref=column(slot),
            send_sem=turn_sem.at[i, p], recv_sem=head_sem.at[slot],
            device_id={"dp": target}, device_id_type=mesh_type,
        )

    def stay(p):
        return pltpu.make_async_copy(
            turned.at[chunks - 1, pl.ds(p * depth, depth)], column(me), keep_sem
        )

    for i in range(chunks):
        keep(i).start()
        for o in range(1, expert_count):
            give(i, (expert + o) % expert_count, expert).start()

    for i in range(chunks):
        k = chunk_of(i)
        keep(i).wait()
        for o in range(1, expert_count):
            peer = (expert + o) % expert_count
            give(i, peer, peer).wait_recv()
        total = jnp.zeros((cols, tok_count), F32)
        for e in range(expert_count):
            total = total + mm(got[k, e], place[e], TN)
        turned[i] = total.astype(BF16)
        for p in range(per):
            target = k * per + p
            if i < chunks - 1:
                hand(i, p, target, me).start()
            else:
                pl.when(me % per != p)(lambda: hand(i, p, target, me).start())
                pl.when(me % per == p)(lambda: stay(p).start())

    for i in range(chunks):
        k = chunk_of(i)
        for o in range(1, expert_count):
            give(i, (expert + o) % expert_count, expert).wait_send()
        for p in range(per):
            target = k * per + p
            if i < chunks - 1:
                hand(i, p, target, me).wait_send()
            else:
                pl.when(me % per != p)(lambda: hand(i, p, target, me).wait_send())
                pl.when(me % per == p)(lambda: stay(p).wait())
    for o in range(1, dp_count):
        peer = (me + o) % dp_count
        hand(0, 0, peer, peer).wait_recv()


def to_heads(expert_count, dp_count, rows, place):
    _, capacity, width = rows.shape
    tok_count = place.shape[2]
    chunks = 4
    cols, depth = width // chunks, width // dp_count
    per = cols // depth
    dma = pltpu.SemaphoreType.DMA
    return pl.pallas_call(
        functools.partial(heads_kernel, expert_count, dp_count),
        out_shape=jax.ShapeDtypeStruct((depth, dp_count * tok_count), BF16),
        in_specs=[
            pl.BlockSpec(memory_space=pl.ANY),
            pl.BlockSpec(memory_space=pltpu.VMEM),
        ],
        out_specs=pl.BlockSpec(memory_space=pl.ANY),
        scratch_shapes=[
            pltpu.VMEM((chunks, expert_count, capacity, cols), BF16),
            pltpu.VMEM((chunks, cols, tok_count), BF16),
            dma((chunks, expert_count)),
            dma((chunks, expert_count)),
            dma((chunks,)),
            dma((chunks, per)),
            dma((dp_count,)),
            dma,
        ],
        cost_estimate=pl.CostEstimate(
            flops=2 * rows.size * tok_count, bytes_accessed=60 * rows.size, transcendentals=0
        ),
        compiler_params=pltpu.CompilerParams(
            collective_id=5, has_side_effects=True, vmem_limit_bytes=32 * 1024 * 1024
        ),
    )(rows, place)


def local(tokens, grad_out, route_ids, route_gates, w_gate, w_up, w_down):
    expert_count = lax.axis_size("expert")
    dp_count = lax.axis_size("dp")
    tok_count = tokens.shape[1]
    width = tokens.shape[2]
    capacity = max(2, 5 * tok_count // (2 * expert_count))
    place = placement(route_ids[0], expert_count, capacity)
    own_grad = grad_out[0].astype(F32)
    gate_column = route_gates[0][:, None]
    scaled_grad = (gate_column * own_grad).astype(BF16)

    def over_experts(rows):
        cols = rows.shape[1]
        got = lax.all_to_all(
            rows.reshape(expert_count, capacity, cols),
            "expert", split_axis=0, concat_axis=0, tiled=True,
        )
        return got.reshape(expert_count * capacity, cols)

    send = jnp.concatenate(
        [
            mm(place, rows).astype(BF16).reshape(expert_count, capacity, width)
            for rows in (tokens[0], scaled_grad)
        ],
        axis=1,
    )
    arrived = lax.all_to_all(send, "expert", split_axis=0, concat_axis=0, tiled=True)
    routed = arrived[:, :capacity].reshape(expert_count * capacity, width)
    routed_grad = arrived[:, capacity:].reshape(expert_count * capacity, width)

    gate_matrix, up_matrix, down_matrix = gather_weights(
        dp_count, (w_gate[0], w_up[0], w_down[0])
    )

    gate_pre = mm(routed, gate_matrix)
    up_pre = mm(routed, up_matrix)
    sigmoid_gate = jax.nn.sigmoid(gate_pre)
    silu_gate = gate_pre * sigmoid_gate
    hidden = (silu_gate * up_pre).astype(BF16)
    expert_out = mm(hidden, down_matrix).astype(BF16)
    hidden_grad = mm(routed_grad, down_matrix, NT)
    expert_out, hidden_grad = lax.optimization_barrier((expert_out, hidden_grad))
    returned = over_experts(expert_out)

    gate_pre_grad = (
        hidden_grad * up_pre * sigmoid_gate * (1.0 + gate_pre * (1.0 - sigmoid_gate))
    ).astype(BF16)
    up_pre_grad = (hidden_grad * silu_gate).astype(BF16)
    input_rows = (mm(gate_pre_grad, gate_matrix, NT) + mm(up_pre_grad, up_matrix, NT)).astype(BF16)
    heads = to_heads(
        expert_count,
        dp_count,
        input_rows.reshape(expert_count, capacity, width),
        place.reshape(expert_count, capacity, tok_count),
    )
    input_grad = heads.T[None]
    token_out = mm(place, returned, TN)
    moe_out = (gate_column * token_out).astype(BF16)
    gate_grad = jnp.sum(own_grad * token_out, axis=1)
    return (moe_out[None], input_grad, gate_grad[None])


def solution(mesh):
    in_specs = (
        P("expert", "dp", None),
        P("expert", "dp", None),
        P("expert", "dp"),
        P("expert", "dp"),
        P("expert", "dp", None),
        P("expert", "dp", None),
        P("expert", "dp", None),
    )
    out_specs = (P("expert", "dp", None), P("expert", None, "dp"), P("expert", "dp"))
    return jax.shard_map(local, mesh=mesh, in_specs=in_specs, out_specs=out_specs, check_vma=False)
```

```python
import functools

import jax
import jax.numpy as jnp
from jax import lax
from jax.experimental import pallas as pl
from jax.experimental.pallas import tpu as pltpu
from jax.sharding import PartitionSpec as P

F32 = jnp.float32
BF16 = jnp.bfloat16


def gather_kernel(dp_count, expert_count, count, kinds, *refs):
    shards, sent = refs[:count], refs[count : count + kinds]
    refs = refs[count + kinds :]
    wholes, got = refs[:count], refs[count : count + kinds]
    right_sem, left_sem, pair_sem, recv_sem, own_sem, give_sem, got_sem, keep_sem = refs[
        count + kinds :
    ]
    expert = lax.axis_index("expert")
    line = dp_count // 2
    me = lax.axis_index("dp")
    z, core = me // 2, me % 2
    pair = z * 2 + (1 - core)
    has_left, has_right = z > 0, z < line - 1

    def greet(target):
        pl.semaphore_signal(
            barrier, inc=1, device_id={"dp": target}, device_id_type=pl.DeviceIdType.MESH
        )

    barrier = pltpu.get_barrier_semaphore()
    greet(pair)
    pl.when(has_left)(lambda: greet(me - 2))
    pl.when(has_right)(lambda: greet(me + 2))
    for o in range(1, expert_count):
        pl.semaphore_signal(
            barrier, inc=1, device_id={"expert": (expert + o) % expert_count},
            device_id_type=pl.DeviceIdType.MESH,
        )
    pl.semaphore_wait(barrier, expert_count + has_left.astype(jnp.int32) + has_right.astype(jnp.int32))

    def block(w, slot):
        rows = shards[w].shape[0]
        return wholes[w].at[pl.ds(pl.multiple_of(slot * rows, rows), rows)]

    def copy(w, slot, sems, step, target, own=False):
        return pltpu.make_async_remote_copy(
            src_ref=shards[w] if own else block(w, slot),
            dst_ref=block(w, slot),
            send_sem=sems.at[w, step],
            recv_sem=recv_sem.at[w, slot],
            device_id={"dp": target},
            device_id_type=pl.DeviceIdType.MESH,
        )

    for w in range(count):
        pl.when(has_right)(lambda: copy(w, me, right_sem, 0, me + 2, True).start())
        pl.when(has_left)(lambda: copy(w, me, left_sem, 0, me - 2, True).start())
        copy(w, me, pair_sem, z, pair, True).start()
        pltpu.make_async_copy(shards[w], block(w, me), own_sem.at[w]).start()

    def give(kind, target, slot):
        return pltpu.make_async_remote_copy(
            src_ref=sent[kind].at[target],
            dst_ref=got[kind].at[slot],
            send_sem=give_sem.at[kind, target],
            recv_sem=got_sem.at[kind, slot],
            device_id={"expert": target},
            device_id_type=pl.DeviceIdType.MESH,
        )

    def keep(kind):
        return pltpu.make_async_copy(
            sent[kind].at[expert], got[kind].at[expert], keep_sem.at[kind]
        )

    for kind in range(kinds):
        keep(kind).start()
        for o in range(1, expert_count):
            give(kind, (expert + o) % expert_count, expert).start()

    for step in range(1, line):
        for w in range(count):
            @pl.when(z >= step)
            def _():
                slot = me - 2 * step
                copy(w, slot, pair_sem, z - step, pair).wait_recv()
                pl.when(has_right)(lambda: copy(w, slot, right_sem, step, me + 2).start())
                copy(w, slot, pair_sem, z - step, pair).start()

            @pl.when(z + step < line)
            def _():
                slot = me + 2 * step
                copy(w, slot, pair_sem, z + step, pair).wait_recv()
                pl.when(has_left)(lambda: copy(w, slot, left_sem, step, me - 2).start())
                copy(w, slot, pair_sem, z + step, pair).start()

    for w in range(count):
        pltpu.make_async_copy(shards[w], block(w, me), own_sem.at[w]).wait()
        for other in range(line):
            copy(w, other * 2 + 1 - core, pair_sem, other, pair).wait_recv()
            copy(w, other * 2 + core, pair_sem, other, pair).wait_send()
        for step in range(line):
            pl.when(has_right & (z >= step))(
                lambda: copy(w, me - 2 * step, right_sem, step, me + 2).wait_send()
            )
            pl.when(has_left & (z + step < line))(
                lambda: copy(w, me + 2 * step, left_sem, step, me - 2).wait_send()
            )
    for kind in range(kinds):
        keep(kind).wait()
        for o in range(1, expert_count):
            peer = (expert + o) % expert_count
            give(kind, peer, expert).wait_send()
            give(kind, peer, peer).wait_recv()


def gather_weights(dp_count, expert_count, shards, sent):
    count, line, kinds = len(shards), dp_count // 2, len(sent)
    hbm = pl.BlockSpec(memory_space=pl.ANY)
    moved = sum(x.size for x in shards) * 2 * dp_count
    return pl.pallas_call(
        functools.partial(gather_kernel, dp_count, expert_count, count, kinds),
        out_shape=[
            jax.ShapeDtypeStruct((dp_count * x.shape[0], x.shape[1]), x.dtype) for x in shards
        ]
        + [jax.ShapeDtypeStruct(x.shape, x.dtype) for x in sent],
        in_specs=[hbm] * (count + kinds),
        out_specs=[hbm] * (count + kinds),
        scratch_shapes=[
            pltpu.SemaphoreType.DMA((count, line)),
            pltpu.SemaphoreType.DMA((count, line)),
            pltpu.SemaphoreType.DMA((count, line)),
            pltpu.SemaphoreType.DMA((count, dp_count)),
            pltpu.SemaphoreType.DMA((count,)),
            pltpu.SemaphoreType.DMA((kinds, expert_count)),
            pltpu.SemaphoreType.DMA((kinds, expert_count)),
            pltpu.SemaphoreType.DMA((kinds,)),
        ],
        cost_estimate=pl.CostEstimate(flops=0, bytes_accessed=moved * 25, transcendentals=0),
        compiler_params=pltpu.CompilerParams(collective_id=3, has_side_effects=True),
    )(*shards, *sent)


def placement(route_line, expert_count, capacity):
    tok_count = route_line.shape[0]
    same = route_line[:, None] == route_line[None, :]
    earlier = jnp.arange(tok_count)[None, :] < jnp.arange(tok_count)[:, None]
    placed = jnp.sum((same & earlier).astype(jnp.int32), axis=1)
    slots = route_line * capacity + placed
    rows = jnp.arange(expert_count * capacity, dtype=jnp.int32)
    return (rows[:, None] == slots[None, :]).astype(BF16)


def mm(a, b, dims=(((1,), (0,)), ((), ()))):
    return lax.dot_general(a, b, dims, preferred_element_type=F32)


NT = (((1,), (1,)), ((), ()))
TN = (((0,), (0,)), ((), ()))


def heads_kernel(expert_count, dp_count, rows, place, out, got, turned, *sems):
    row_sem, got_sem, own_sem, turn_sem, head_sem, keep_sem = sems
    expert, me = lax.axis_index("expert"), lax.axis_index("dp")
    chunks, cols = got.shape[0], got.shape[3]
    depth, tok_count = out.shape[0], place.shape[2]
    per = cols // depth
    mesh_type = pl.DeviceIdType.MESH

    barrier = pltpu.get_barrier_semaphore()
    for o in range(1, expert_count):
        pl.semaphore_signal(
            barrier, inc=1, device_id={"expert": (expert + o) % expert_count},
            device_id_type=mesh_type,
        )
    for o in range(1, dp_count):
        pl.semaphore_signal(
            barrier, inc=1, device_id={"dp": (me + o) % dp_count}, device_id_type=mesh_type
        )
    pl.semaphore_wait(barrier, expert_count + dp_count - 2)

    def chunk_of(i):
        return (me // per + 1 + i) % chunks

    def source(k, e):
        return rows.at[e, :, pl.ds(pl.multiple_of(k * cols, 128), cols)]

    def give(i, target, slot):
        k = chunk_of(i)
        return pltpu.make_async_remote_copy(
            src_ref=source(k, target), dst_ref=got.at[k, slot],
            send_sem=row_sem.at[i, target], recv_sem=got_sem.at[i, slot],
            device_id={"expert": target}, device_id_type=mesh_type,
        )

    def keep(i):
        k = chunk_of(i)
        return pltpu.make_async_copy(source(k, expert), got.at[k, expert], own_sem.at[i])

    def column(slot):
        return out.at[:, pl.ds(pl.multiple_of(slot * tok_count, 128), tok_count)]

    def hand(i, p, target, slot):
        return pltpu.make_async_remote_copy(
            src_ref=turned.at[i, pl.ds(p * depth, depth)], dst_ref=column(slot),
            send_sem=turn_sem.at[i, p], recv_sem=head_sem.at[slot],
            device_id={"dp": target}, device_id_type=mesh_type,
        )

    def stay(p):
        return pltpu.make_async_copy(
            turned.at[chunks - 1, pl.ds(p * depth, depth)], column(me), keep_sem
        )

    for i in range(chunks):
        keep(i).start()
        for o in range(1, expert_count):
            give(i, (expert + o) % expert_count, expert).start()

    for i in range(chunks):
        k = chunk_of(i)
        keep(i).wait()
        for o in range(1, expert_count):
            peer = (expert + o) % expert_count
            give(i, peer, peer).wait_recv()
        total = jnp.zeros((cols, tok_count), F32)
        for e in range(expert_count):
            total = total + mm(got[k, e], place[e], TN)
        turned[i] = total.astype(BF16)
        for p in range(per):
            target = k * per + p
            if i < chunks - 1:
                hand(i, p, target, me).start()
            else:
                pl.when(me % per != p)(lambda: hand(i, p, target, me).start())
                pl.when(me % per == p)(lambda: stay(p).start())

    for i in range(chunks):
        k = chunk_of(i)
        for o in range(1, expert_count):
            give(i, (expert + o) % expert_count, expert).wait_send()
        for p in range(per):
            target = k * per + p
            if i < chunks - 1:
                hand(i, p, target, me).wait_send()
            else:
                pl.when(me % per != p)(lambda: hand(i, p, target, me).wait_send())
                pl.when(me % per == p)(lambda: stay(p).wait())
    for o in range(1, dp_count):
        peer = (me + o) % dp_count
        hand(0, 0, peer, peer).wait_recv()


def to_heads(expert_count, dp_count, rows, place):
    _, capacity, width = rows.shape
    tok_count = place.shape[2]
    chunks = 4
    cols, depth = width // chunks, width // dp_count
    per = cols // depth
    dma = pltpu.SemaphoreType.DMA
    return pl.pallas_call(
        functools.partial(heads_kernel, expert_count, dp_count),
        out_shape=jax.ShapeDtypeStruct((depth, dp_count * tok_count), BF16),
        in_specs=[
            pl.BlockSpec(memory_space=pl.ANY),
            pl.BlockSpec(memory_space=pltpu.VMEM),
        ],
        out_specs=pl.BlockSpec(memory_space=pl.ANY),
        scratch_shapes=[
            pltpu.VMEM((chunks, expert_count, capacity, cols), BF16),
            pltpu.VMEM((chunks, cols, tok_count), BF16),
            dma((chunks, expert_count)),
            dma((chunks, expert_count)),
            dma((chunks,)),
            dma((chunks, per)),
            dma((dp_count,)),
            dma,
        ],
        cost_estimate=pl.CostEstimate(
            flops=2 * rows.size * tok_count, bytes_accessed=60 * rows.size, transcendentals=0
        ),
        compiler_params=pltpu.CompilerParams(
            collective_id=5, has_side_effects=True, vmem_limit_bytes=32 * 1024 * 1024
        ),
    )(rows, place)


def local(tokens, grad_out, route_ids, route_gates, w_gate, w_up, w_down):
    expert_count = lax.axis_size("expert")
    dp_count = lax.axis_size("dp")
    tok_count = tokens.shape[1]
    width = tokens.shape[2]
    capacity = max(2, 5 * tok_count // (2 * expert_count))
    place = placement(route_ids[0], expert_count, capacity)
    own_grad = grad_out[0].astype(F32)
    gate_column = route_gates[0][:, None]
    scaled_grad = (gate_column * own_grad).astype(BF16)

    def over_experts(rows):
        cols = rows.shape[1]
        got = lax.all_to_all(
            rows.reshape(expert_count, capacity, cols),
            "expert", split_axis=0, concat_axis=0, tiled=True,
        )
        return got.reshape(expert_count * capacity, cols)

    sent = [
        mm(place, rows).astype(BF16).reshape(expert_count, capacity, width)
        for rows in (tokens[0], scaled_grad)
    ]
    gate_matrix, up_matrix, down_matrix, routed, routed_grad = gather_weights(
        dp_count, expert_count, (w_gate[0], w_up[0], w_down[0]), sent
    )
    routed = routed.reshape(expert_count * capacity, width)
    routed_grad = routed_grad.reshape(expert_count * capacity, width)

    gate_pre = mm(routed, gate_matrix)
    up_pre = mm(routed, up_matrix)
    sigmoid_gate = jax.nn.sigmoid(gate_pre)
    silu_gate = gate_pre * sigmoid_gate
    hidden = (silu_gate * up_pre).astype(BF16)
    expert_out = mm(hidden, down_matrix).astype(BF16)
    hidden_grad = mm(routed_grad, down_matrix, NT)
    expert_out, hidden_grad = lax.optimization_barrier((expert_out, hidden_grad))
    returned = over_experts(expert_out)

    gate_pre_grad = (
        hidden_grad * up_pre * sigmoid_gate * (1.0 + gate_pre * (1.0 - sigmoid_gate))
    ).astype(BF16)
    up_pre_grad = (hidden_grad * silu_gate).astype(BF16)
    input_rows = (mm(gate_pre_grad, gate_matrix, NT) + mm(up_pre_grad, up_matrix, NT)).astype(BF16)
    heads = to_heads(
        expert_count,
        dp_count,
        input_rows.reshape(expert_count, capacity, width),
        place.reshape(expert_count, capacity, tok_count),
    )
    input_grad = heads.T[None]
    token_out = mm(place, returned, TN)
    moe_out = (gate_column * token_out).astype(BF16)
    gate_grad = jnp.sum(own_grad * token_out, axis=1)
    return (moe_out[None], input_grad, gate_grad[None])


def solution(mesh):
    in_specs = (
        P("expert", "dp", None),
        P("expert", "dp", None),
        P("expert", "dp"),
        P("expert", "dp"),
        P("expert", "dp", None),
        P("expert", "dp", None),
        P("expert", "dp", None),
    )
    out_specs = (P("expert", "dp", None), P("expert", None, "dp"), P("expert", "dp"))
    return jax.shard_map(local, mesh=mesh, in_specs=in_specs, out_specs=out_specs, check_vma=False)
```
